32 devices in a mesh: parts: 2 (over x), tensor: 8 (over z, y), section: 2 (over core).
Axes of the slice: x: 2, y: 2, z: 4, core: 2. Of those that a mesh axis runs over, the one named last changes fastest.
Arguments:
- tokens: bfloat16 [2048, 8192], P(('parts', 'section'), 'tensor'), parts along dimension 0
- decode_hidden_rows: bfloat16 [2048, 8192], P(('parts', 'section'), 'tensor'), parts along dimension 0
- query_matrix: bfloat16 [8192, 8192], P(None, 'tensor'), may hold values from -0.0625 to 0.0625
- key_value_matrix: bfloat16 [8192, 2048], P(None, 'tensor'), may hold values from -0.0625 to 0.0625
- adapter_slot_pool: bfloat16 [16, 8192, 128], P('tensor'), may hold values from -0.0625 to 0.0625
- adapter_slot_map: int32 [16], replicated, may hold values from 0 to 15, each once
- tenant_adapter_index: int32 [16], P(('parts', 'section')), parts along dimension 0, may hold values from 0 to 15
- decode_page_table: int32 [2048, 32], P(('parts', 'section')), parts along dimension 0, may hold values from 0 to 63, as said below
- lengths: int32 [2048], P(('parts', 'section')), parts along dimension 0, may hold values from 1 to 512, as said below
Outputs:
- prefill_heads: bfloat16 [2048, 8192], P(('parts', 'section'), 'tensor'), parts along dimension 0
- decode_heads: bfloat16 [2048, 8192], P(('parts', 'section'), 'tensor'), parts along dimension 0
The draws below stay inside these ranges and needn't reach their ends.
There are 2 independent parts, one for each index of `parts`. The reference program is written for one: setup_inputs(seed, part) draws one part's arguments, and reference() takes and returns one part's arrays. A program takes and returns all parts, laid end to end along the dimension named above; an argument that names none is the same for every part. Nothing has to cross between parts.
Inputs may be any that keep to these rules, and one draw needn't show every extreme that they name: `adapter_slot_map`: each slot 0 to 15 once; slot s lies on index s // 2 of tensor. `decode_page_table`: the 32 pages of a row are distinct. `lengths`: some row has the full length.
All inputs are finite; a program needn't handle non-finite values.
Results may differ from the reference program's by a relative error of at most 0.0045.
The reference program's roundings to bfloat16 on the way count: a program that leaves them out, or rounds other values in their place, can miss the bound.
Values may be sent and summed in bfloat16 or wider, within the bound.
A program may use at most 192 MiB of HBM per device.

```python
import math
import jax
import jax.numpy as jnp
import numpy as np
from jax import lax

MODEL_WIDTH = 8192
HQ = 64
KVH = 8
HD = 128
ADAPTER_RANK = 64
CTOK = 128
STRETCHES = 8
PTOK = 1024
ADAPTER_POOL = 16
PAGE = 16
PPR = 32
NPAGES = 64
DROWS = 1024


def draw_tokens(key, part):
    key = jax.random.fold_in(key, 21)
    values = jax.random.normal(key, (PTOK, MODEL_WIDTH), jnp.float32)
    return values.astype(jnp.bfloat16)


def draw_decode_hidden_rows(key, part):
    key = jax.random.fold_in(key, 22)
    values = jax.random.normal(key, (DROWS, MODEL_WIDTH), jnp.float32)
    return values.astype(jnp.bfloat16)


def draw_decode_page_table(key, part):
    key = jax.random.fold_in(key, 23)
    scores = jax.random.randint(key, (DROWS, NPAGES), 0, 65536, jnp.int32) * NPAGES + jnp.arange(NPAGES, dtype=jnp.int32)[None, :]
    order = jnp.argsort(scores, axis=1, stable=True).astype(jnp.int32)
    return order[:, :PPR]


def draw_lengths(key, part):
    key = jax.random.fold_in(key, 24)
    first, second, third, fourth = jax.random.split(key, 4)
    longest = PPR * PAGE
    one = jax.random.randint(first, (DROWS,), 1, longest + 1, jnp.int32)
    two = jax.random.randint(second, (DROWS,), 1, longest + 1, jnp.int32)
    three = jax.random.randint(third, (DROWS,), 1, longest + 1, jnp.int32)
    values = jnp.minimum(jnp.minimum(one, two), three)
    chosen = jax.random.randint(fourth, (), 0, DROWS, jnp.int32)
    return values.at[chosen].set(longest)


def touch_ends(values, own_key, least, high):
    spot = [jax.random.randint(jax.random.fold_in(own_key, axis), (), 0, length) for axis, length in enumerate(values.shape)]
    widest = values.shape.index(max(values.shape))
    neighbour = spot[:widest] + [(spot[widest] + 1) % values.shape[widest]] + spot[widest + 1:]
    return values.at[tuple(spot)].set(least).at[tuple(neighbour)].set(high)


def block_levels(rng, shape, shards, smallest, largest):
    loudness = 1.0
    for dim, blocks in shards:
        draws = jax.random.uniform(jax.random.fold_in(jax.random.fold_in(rng, 6), dim), (blocks,), jnp.float32, smallest / len(shards), largest / len(shards))
        loudness = loudness * jnp.repeat(jnp.exp(draws), shape[dim] // blocks).reshape((-1,) + (1,) * (len(shape) - 1 - dim))
    return loudness


def cumulative_ranks(amount, lean):
    loads = [(1 << 20) // math.isqrt(grade ** lean) + 1 for grade in range(1, amount + 1)]
    scale = 1 + sum(loads) // (1 << 30)
    return np.cumsum(np.array([max(1, weight // scale) for weight in loads]))


def ranked_ids(own_key, shape, amount, skew):
    grid = cumulative_ranks(amount, skew)
    ticket = jax.random.randint(jax.random.fold_in(own_key, 1), shape, 0, int(grid[amount - 1]))
    grade = jnp.searchsorted(jnp.asarray(grid, jnp.int32), ticket, side="right")
    return jax.random.permutation(jax.random.fold_in(own_key, 2), amount)[grade].astype(jnp.int32)


def centred(own_key, shape, spread, limit, cuts=(), held_as=jnp.bfloat16):
    drawn = spread * jax.random.normal(own_key, shape, jnp.float32)
    if cuts:
        drawn = drawn * block_levels(own_key, shape, cuts, -0.22, 0.18)
    return jnp.clip(drawn, -limit, limit).astype(held_as)


def setup_inputs(seed: int = 0, part: int = 0) -> dict:
    streams_of = jax.random.split(jax.random.key(seed), 10)
    own_keys = jax.random.split(jax.random.fold_in(streams_of[9], part), 10)
    return {
        "tokens": draw_tokens(jax.random.fold_in(jax.random.fold_in(streams_of[9], part), 71), part),
        "decode_hidden_rows": draw_decode_hidden_rows(jax.random.fold_in(jax.random.fold_in(streams_of[9], part), 71), part),
        "query_matrix": centred(streams_of[2], (MODEL_WIDTH, MODEL_WIDTH), MODEL_WIDTH ** -0.5, 0.0625, ((1, 8),)),
        "key_value_matrix": centred(streams_of[3], (MODEL_WIDTH, 2 * KVH * HD), MODEL_WIDTH ** -0.5, 0.0625, ((1, 8),)),
        "adapter_slot_pool": centred(streams_of[4], (ADAPTER_POOL, MODEL_WIDTH, 2 * ADAPTER_RANK), MODEL_WIDTH ** -0.5, 0.0625, ((0, 8),)),
        "adapter_slot_map": jax.random.permutation(streams_of[5], ADAPTER_POOL).astype(jnp.int32),
        "tenant_adapter_index": touch_ends(ranked_ids(own_keys[6], (STRETCHES,), ADAPTER_POOL, 2), jax.random.fold_in(own_keys[6], 3), 0, ADAPTER_POOL - 1).astype(jnp.int32),
        "decode_page_table": draw_decode_page_table(jax.random.fold_in(jax.random.fold_in(streams_of[9], part), 71), part),
        "lengths": draw_lengths(jax.random.fold_in(jax.random.fold_in(streams_of[9], part), 71), part),
    }


ADAPTER_SCALE = 2.0

def reference(tokens, decode_hidden_rows, query_matrix, key_value_matrix, adapter_slot_pool, adapter_slot_map, tenant_adapter_index, decode_page_table, lengths):
    scale = 1.0 / math.sqrt(HD)
    group = HQ // KVH
    key_cols = KVH * HD
    tok_count = tokens.shape[0]
    stretch_count = tok_count // CTOK
    row_count = decode_hidden_rows.shape[0]
    pool_slots = adapter_slot_map[tenant_adapter_index]
    adapter_list = adapter_slot_pool[pool_slots].astype(jnp.float32)
    blocks = tokens.reshape(stretch_count, CTOK, MODEL_WIDTH).astype(jnp.float32)
    low_rank = jnp.einsum('ctd,cdr->ctr', blocks, adapter_list[:, :, :ADAPTER_RANK]).astype(jnp.bfloat16)
    adapter_update = jnp.einsum('ctr,cdr->ctd', low_rank.astype(jnp.float32), adapter_list[:, :, ADAPTER_RANK:]).reshape(tok_count, MODEL_WIDTH)
    query_token_rows = (jnp.dot(tokens, query_matrix, preferred_element_type=jnp.float32) + ADAPTER_SCALE * adapter_update).astype(jnp.bfloat16)
    keyval_tok = jnp.dot(tokens, key_value_matrix, preferred_element_type=jnp.float32).astype(jnp.bfloat16)
    query_dec = jnp.dot(decode_hidden_rows, query_matrix, preferred_element_type=jnp.float32).astype(jnp.bfloat16)
    keyval_dec = jnp.dot(decode_hidden_rows, key_value_matrix, preferred_element_type=jnp.float32).astype(jnp.bfloat16)
    query_five = query_token_rows.reshape(stretch_count, CTOK, KVH, group, HD).astype(jnp.float32)
    keys_four = keyval_tok[:, :key_cols].reshape(stretch_count, CTOK, KVH, HD).astype(jnp.float32)
    vals_four = keyval_tok[:, key_cols:].reshape(stretch_count, CTOK, KVH, HD).astype(jnp.float32)
    scores = jnp.einsum('ctkgd,cskd->ckgts', query_five, keys_four) * scale
    causal = jnp.arange(CTOK)[:, None] >= jnp.arange(CTOK)[None, :]
    scores = jnp.where(causal, scores, -jnp.inf)
    peak = lax.optimization_barrier(jnp.max(scores, axis=-1, keepdims=True))
    expo = jnp.exp(scores - peak)
    weights = (expo / lax.optimization_barrier(jnp.sum(expo, axis=-1, keepdims=True))).astype(jnp.bfloat16)
    prefill_heads = jnp.einsum('ckgts,cskd->ctkgd', weights.astype(jnp.float32), vals_four).astype(jnp.bfloat16).reshape(tok_count, MODEL_WIDTH)
    page_count = tok_count // PAGE
    match = decode_page_table[:, :, None] == jnp.arange(page_count, dtype=jnp.int32)[None, None, :]
    present = jnp.any(match, axis=1)
    place = lax.optimization_barrier(jnp.sum(jnp.where(match, jnp.arange(PPR, dtype=jnp.int32)[None, :, None], 0), axis=1)).astype(jnp.int32)
    keypos = place[:, :, None] * PAGE + jnp.arange(PAGE, dtype=jnp.int32)[None, None, :]
    live = (present[:, :, None] & (keypos < lengths[:, None, None])).reshape(row_count, tok_count)
    query_four = query_dec.reshape(row_count, KVH, group, HD).astype(jnp.float32)
    ctx_keys = keyval_tok[:, :key_cols].reshape(tok_count, KVH, HD).astype(jnp.float32)
    ctx_vals = keyval_tok[:, key_cols:].reshape(tok_count, KVH, HD).astype(jnp.float32)
    self_keys = keyval_dec[:, :key_cols].reshape(row_count, KVH, HD).astype(jnp.float32)
    self_vals = keyval_dec[:, key_cols:].reshape(row_count, KVH, HD).astype(jnp.float32)
    outputs = []
    for head in range(KVH):
        query_g = query_four[:, head]
        dec_scores = jnp.einsum('rgd,nd->rgn', query_g, ctx_keys[:, head]) * scale
        own_score = jnp.einsum('rgd,rd->rg', query_g, self_keys[:, head]) * scale
        dec_scores = jnp.where(live[:, None, :], dec_scores, -jnp.inf)
        top = jnp.maximum(lax.optimization_barrier(jnp.max(dec_scores, axis=-1)), own_score)
        dec_exp = jnp.exp(dec_scores - top[..., None])
        own_exp = jnp.exp(own_score - top)
        total = lax.optimization_barrier(jnp.sum(dec_exp, axis=-1)) + own_exp
        dec_weights = (dec_exp / total[..., None]).astype(jnp.bfloat16)
        own_weight = (own_exp / total).astype(jnp.bfloat16)
        result = jnp.einsum('rgn,nd->rgd', dec_weights.astype(jnp.float32), ctx_vals[:, head])
        result = result + own_weight.astype(jnp.float32)[..., None] * self_vals[:, head][:, None, :]
        outputs.append(result.astype(jnp.bfloat16))
    decode_heads = jnp.stack(outputs, axis=1).reshape(row_count, MODEL_WIDTH)
    return (prefill_heads, decode_heads)
```

```python
import functools
import math

import jax
import jax.numpy as jnp
from jax import lax
from jax.experimental import pallas as pl
from jax.experimental.pallas import tpu as pltpu
from jax.sharding import PartitionSpec as P

HQ = 64
KVH = 8
HD = 128
ADAPTER_RANK = 64
CTOK = 128
POOL_PER_INDEX = 2
PAGE = 16
PPR = 32
ADAPTER_SCALE = 2.0
SCALE = 1.0 / math.sqrt(HD)
GROUP = HQ // KVH


def dot_t(a, b):
    return lax.dot_general(a, b, (((1,), (1,)), ((), ())), preferred_element_type=jnp.float32)


def attention_kernel(qt, qd, kt, vt, kc, vc, ks, vs, bias, out_t, out_d):
    causal = lax.broadcasted_iota(jnp.int32, (CTOK, CTOK), 0) >= lax.broadcasted_iota(
        jnp.int32, (CTOK, CTOK), 1
    )
    for c in range(qt.shape[0] // CTOK):
        rows = pl.ds(c * CTOK, CTOK)
        scores = jnp.where(causal, dot_t(qt[rows, :], kt[rows, :]) * SCALE, -jnp.inf)
        expo = jnp.exp(scores - jnp.max(scores, axis=-1, keepdims=True))
        weights = (expo / jnp.sum(expo, axis=-1, keepdims=True)).astype(jnp.bfloat16)
        result = jnp.dot(weights, vt[rows, :], preferred_element_type=jnp.float32)
        out_t[rows, :] = result.astype(jnp.bfloat16)
    tile = min(128, qd.shape[0])
    for r in range(qd.shape[0] // tile):
        rows = pl.ds(r * tile, tile)
        query = qd[rows, :]
        scores = dot_t(query, kc[...]) * SCALE + bias[rows, :].astype(jnp.float32)
        own = (
            jnp.sum(
                query.astype(jnp.float32) * ks[rows, :].astype(jnp.float32), axis=-1, keepdims=True
            )
            * SCALE
        )
        top = jnp.maximum(jnp.max(scores, axis=-1, keepdims=True), own)
        expo = jnp.exp(scores - top)
        own_exp = jnp.exp(own - top)
        total = jnp.sum(expo, axis=-1, keepdims=True) + own_exp
        weights = (expo / total).astype(jnp.bfloat16)
        own_weight = (own_exp / total).astype(jnp.bfloat16).astype(jnp.float32)
        result = jnp.dot(weights, vc[...], preferred_element_type=jnp.float32)
        result = result + own_weight * vs[rows, :].astype(jnp.float32)
        out_d[rows, :] = result.astype(jnp.bfloat16)


def attention(query_tok, query_dec, keys_tok, vals_tok, keys_ctx, vals_ctx, self_k, self_v, bias):
    heads = query_tok.shape[1] // HD

    def per_head(rows):
        return pl.BlockSpec((rows, HD), lambda i: (0, i))

    def per_group(array):
        return pl.BlockSpec((array.shape[0], HD), lambda i: (0, i // GROUP))

    shared = (keys_tok, vals_tok, keys_ctx, vals_ctx, self_k, self_v)
    return pl.pallas_call(
        attention_kernel,
        grid=(heads,),
        in_specs=[
            per_head(query_tok.shape[0]),
            per_head(query_dec.shape[0]),
            *[per_group(a) for a in shared],
            pl.BlockSpec(bias.shape, lambda i: (0, 0)),
        ],
        out_specs=[per_head(query_tok.shape[0]), per_head(query_dec.shape[0])],
        out_shape=[
            jax.ShapeDtypeStruct(query_tok.shape, jnp.bfloat16),
            jax.ShapeDtypeStruct(query_dec.shape, jnp.bfloat16),
        ],
        compiler_params=pltpu.CompilerParams(vmem_limit_bytes=32 * 1024 * 1024),
    )(query_tok, query_dec, *shared, bias)


def live_bias(decode_page_table, lengths, page_count):
    match = decode_page_table[:, :, None] == jnp.arange(page_count, dtype=jnp.int32)[None, None, :]
    place = jnp.max(jnp.where(match, jnp.arange(PPR, dtype=jnp.int32)[None, :, None], -1), axis=1)
    left = jnp.where(place >= 0, lengths[:, None] - place * PAGE, 0)
    live = jnp.arange(PAGE, dtype=jnp.int32)[None, None, :] < left[:, :, None]
    bias = jnp.where(live, 0.0, -jnp.inf).astype(jnp.bfloat16)
    return bias.reshape(lengths.shape[0], page_count * PAGE)


def own_heads(keyval_mine, heads_here):
    index = lax.axis_index("tensor")
    if heads_here == GROUP and keyval_mine.shape[1] == 2 * HD:
        half = KVH // 2
        first, second = keyval_mine[:, :HD], keyval_mine[:, HD:]
        holds_keys = index < half
        one = lax.ppermute(
            jnp.where(holds_keys, first, second),
            "tensor",
            [(j, 2 * j) for j in range(half)] + [(half + j, 2 * j + 1) for j in range(half)],
        )
        two = lax.ppermute(
            jnp.where(holds_keys, second, first),
            "tensor",
            [(j, 2 * j + 1) for j in range(half)] + [(half + j, 2 * j) for j in range(half)],
        )
        even = index % 2 == 0
        return jnp.where(even, one, two), jnp.where(even, two, one)
    kv_here = max(1, heads_here // GROUP)
    whole = lax.all_gather(keyval_mine, "tensor", axis=1, tiled=True)
    first = index * heads_here // GROUP
    return (
        lax.dynamic_slice_in_dim(whole, first * HD, kv_here * HD, 1),
        lax.dynamic_slice_in_dim(whole, (KVH + first) * HD, kv_here * HD, 1),
    )


def on_device(
    tokens,
    decode_hidden_rows,
    query_matrix,
    key_value_matrix,
    adapter_slot_pool,
    adapter_slot_map,
    tenant_adapter_index,
    decode_page_table,
    lengths,
):
    token_rows = tokens.shape[0]
    heads_here = query_matrix.shape[1] // HD
    stretches = token_rows // CTOK
    index = lax.axis_index("tensor")
    slots = adapter_slot_map[tenant_adapter_index]

    up = jnp.swapaxes(adapter_slot_pool[:, :, ADAPTER_RANK:], 1, 2)
    up_all = lax.all_to_all(up, "tensor", split_axis=2, concat_axis=0, tiled=True)
    tokens_all = lax.all_gather(tokens, "tensor", axis=1, tiled=True)
    rows_all = lax.all_gather(decode_hidden_rows, "tensor", axis=1, tiled=True)

    low_local = jnp.einsum(
        "td,sdr->str",
        tokens_all,
        adapter_slot_pool[:, :, :ADAPTER_RANK],
        preferred_element_type=jnp.float32,
    )
    query_sum = jnp.dot(tokens_all, query_matrix, preferred_element_type=jnp.float32)
    keyval_tok = jnp.dot(tokens_all, key_value_matrix, preferred_element_type=jnp.float32)
    query_dec = jnp.dot(rows_all, query_matrix, preferred_element_type=jnp.float32)
    keyval_dec = jnp.dot(rows_all, key_value_matrix, preferred_element_type=jnp.float32)

    low_local = low_local.reshape(POOL_PER_INDEX, stretches, CTOK, ADAPTER_RANK)
    held = index * POOL_PER_INDEX + jnp.arange(POOL_PER_INDEX, dtype=jnp.int32)
    mine = held[:, None] == slots[None, :]
    low_mine = jnp.sum(jnp.where(mine[:, :, None, None], low_local, 0.0), axis=0)
    low = lax.psum(low_mine.astype(jnp.bfloat16), "tensor")
    update = jnp.einsum("ctr,crd->ctd", low, up_all[slots], preferred_element_type=jnp.float32)
    update = update.reshape(token_rows, query_matrix.shape[1])
    query_tok = (query_sum + ADAPTER_SCALE * update).astype(jnp.bfloat16)

    keyval_mine = jnp.concatenate((keyval_tok, keyval_dec), axis=0).astype(jnp.bfloat16)
    keys, vals = own_heads(keyval_mine, heads_here)
    keys_ctx = lax.all_gather(keys[:token_rows], "section", axis=0, tiled=True)
    vals_ctx = lax.all_gather(vals[:token_rows], "section", axis=0, tiled=True)
    bias = live_bias(decode_page_table, lengths, keys_ctx.shape[0] // PAGE)
    return tuple(
        attention(
            query_tok,
            query_dec.astype(jnp.bfloat16),
            keys[:token_rows],
            vals[:token_rows],
            keys_ctx,
            vals_ctx,
            keys[token_rows:],
            vals[token_rows:],
            bias,
        )
    )


def solution(mesh):
    placed = (
        P(("parts", "section"), "tensor"),
        P(("parts", "section"), "tensor"),
        P(None, "tensor"),
        P(None, "tensor"),
        P("tensor", None, None),
        P(),
        P(("parts", "section")),
        P(("parts", "section"), None),
        P(("parts", "section")),
    )
    return jax.shard_map(
        on_device,
        mesh=mesh,
        in_specs=placed,
        out_specs=(P(("parts", "section"), "tensor"), P(("parts", "section"), "tensor")),
        check_vma=False,
    )
```

```python
import functools
import math

import jax
import jax.numpy as jnp
from jax import lax
from jax.experimental import pallas as pl
from jax.experimental.pallas import tpu as pltpu
from jax.sharding import PartitionSpec as P

HQ = 64
KVH = 8
HD = 128
ADAPTER_RANK = 64
CTOK = 128
POOL_PER_INDEX = 2
PAGE = 16
PPR = 32
ADAPTER_SCALE = 2.0
SCALE = 1.0 / math.sqrt(HD)
GROUP = HQ // KVH


def dot_t(a, b):
    return lax.dot_general(a, b, (((1,), (1,)), ((), ())), preferred_element_type=jnp.float32)


def attention_kernel(qt, qd, kt, vt, kc, vc, ks, vs, bias, out_t, out_d):
    causal = lax.broadcasted_iota(jnp.int32, (CTOK, CTOK), 0) >= lax.broadcasted_iota(
        jnp.int32, (CTOK, CTOK), 1
    )
    for c in range(qt.shape[0] // CTOK):
        rows = pl.ds(c * CTOK, CTOK)
        scores = jnp.where(causal, dot_t(qt[rows, :], kt[rows, :]) * SCALE, -jnp.inf)
        expo = jnp.exp(scores - jnp.max(scores, axis=-1, keepdims=True))
        weights = (expo / jnp.sum(expo, axis=-1, keepdims=True)).astype(jnp.bfloat16)
        result = jnp.dot(weights, vt[rows, :], preferred_element_type=jnp.float32)
        out_t[rows, :] = result.astype(jnp.bfloat16)
    tile = min(128, qd.shape[0])
    for r in range(qd.shape[0] // tile):
        rows = pl.ds(r * tile, tile)
        query = qd[rows, :]
        scores = dot_t(query, kc[...]) * SCALE + bias[rows, :].astype(jnp.float32)
        own = (
            jnp.sum(
                query.astype(jnp.float32) * ks[rows, :].astype(jnp.float32), axis=-1, keepdims=True
            )
            * SCALE
        )
        top = jnp.maximum(jnp.max(scores, axis=-1, keepdims=True), own)
        expo = jnp.exp(scores - top)
        own_exp = jnp.exp(own - top)
        total = jnp.sum(expo, axis=-1, keepdims=True) + own_exp
        weights = (expo / total).astype(jnp.bfloat16)
        own_weight = (own_exp / total).astype(jnp.bfloat16).astype(jnp.float32)
        result = jnp.dot(weights, vc[...], preferred_element_type=jnp.float32)
        result = result + own_weight * vs[rows, :].astype(jnp.float32)
        out_d[rows, :] = result.astype(jnp.bfloat16)


def attention(query_tok, query_dec, keys_tok, vals_tok, keys_ctx, vals_ctx, self_k, self_v, bias):
    heads = query_tok.shape[1] // HD

    def per_head(rows):
        return pl.BlockSpec((rows, HD), lambda i: (0, i))

    def per_group(array):
        return pl.BlockSpec((array.shape[0], HD), lambda i: (0, i // GROUP))

    shared = (keys_tok, vals_tok, keys_ctx, vals_ctx, self_k, self_v)
    return pl.pallas_call(
        attention_kernel,
        grid=(heads,),
        in_specs=[
            per_head(query_tok.shape[0]),
            per_head(query_dec.shape[0]),
            *[per_group(a) for a in shared],
            pl.BlockSpec(bias.shape, lambda i: (0, 0)),
        ],
        out_specs=[per_head(query_tok.shape[0]), per_head(query_dec.shape[0])],
        out_shape=[
            jax.ShapeDtypeStruct(query_tok.shape, jnp.bfloat16),
            jax.ShapeDtypeStruct(query_dec.shape, jnp.bfloat16),
        ],
        compiler_params=pltpu.CompilerParams(vmem_limit_bytes=32 * 1024 * 1024),
    )(query_tok, query_dec, *shared, bias)


def link_orders():
    sent, links, arrived = {}, {}, {z: [(0, (z, 0, 0)), (0, (z, 0, 1))] for z in range(4)}
    events = [(0, z, (z, 0, h)) for h in range(2) for z in range(4)]
    while events:
        events.sort(key=lambda e: (e[0], e[2][1], abs(e[2][0] - e[1]), e[2][2], e[1]))
        time, z, unit = events.pop(0)
        source, side, half = unit
        out = []
        if side == 0:
            if source <= z < 3:
                out.append(("up", z + 1, unit, time))
            if source >= z > 0:
                out.append(("down", z - 1, unit, time))
            if not (source == (z ^ 1) and half == 0):
                out.append(("y", z, (source, 1, half), time))
        elif source == z and half == 0:
            way = "up" if (z ^ 1) > z else "down"
            out.append(("ext", z ^ 1, (z, 1, 0), max(time, 4.5) if z in (1, 2) else time))
        for kind, place, name, ready in out:
            link = (z, place)
            done = max(links.get(link, 0), ready) + 1
            if kind != "ext" or z not in (1, 2):
                links[link] = done
            else:
                done = 7
            sent.setdefault((z, unit), []).append(kind)
            arrived[place].append((done, name))
            if kind != "ext":
                events.append((done, place, name))
    tables = []
    for z in range(4):
        order = [name for _, name in sorted(arrived[z], key=lambda e: (e[0], e[1][1]))]
        last = max(i for i, u in enumerate(order) if {"up", "down"} & set(sent.get((z, u), [])))
        row = []
        for i, unit in enumerate(order):
            kinds = sent.get((z, unit), [])
            flags = sum(bit for kind, bit in (("up", 1), ("down", 2), ("y", 4)) if kind in kinds)
            late = order.index((z, 1, 0))
            if i == max(last, late):
                flags += 8
            row.append(flags * 16 + unit[0] * 4 + unit[1] * 2 + unit[2])
        tables.append(row)
    return tables


def project_kernel(
    tok, dec, wq, wkv, pool, q_out, kv_out, low_out, up_out,
    x, w, wk, ad, up_send, up_all, local_sem, send_sem, recv_sem, up_ssem, up_rsem, pair_sem,
):
    tables = link_orders()
    me = lax.axis_index("tensor")
    core = lax.axis_index("section")
    z, y = me // 2, me % 2
    rows, width = tok.shape

    own = [
        pltpu.make_async_copy(tok, x.at[me, 0], local_sem.at[0]),
        pltpu.make_async_copy(dec, x.at[me, 1], local_sem.at[1]),
    ]
    loads = [
        pltpu.make_async_copy(pool, ad, local_sem.at[2]),
        pltpu.make_async_copy(wkv, wk, local_sem.at[3]),
        pltpu.make_async_copy(wq, w, local_sem.at[4]),
    ]
    for copy in own + loads:
        copy.start()

    barrier = pltpu.get_barrier_semaphore()
    for k in range(1, 8):
        pl.semaphore_signal(
            barrier, inc=1, device_id={"tensor": (me + k) % 8}, device_id_type=pl.DeviceIdType.MESH
        )
    pl.semaphore_signal(
        barrier, inc=1, device_id={"section": 1 - core}, device_id_type=pl.DeviceIdType.MESH
    )
    pl.semaphore_wait(barrier, 8)
    for copy in own:
        copy.wait()

    def decode(i):
        code = jnp.int32(0)
        for place in range(4):
            for step in range(16):
                here = jnp.logical_and(z == place, i == step)
                code = jnp.where(here, tables[place][step], code)
        unit, flags = code % 16, code // 16
        slot = (unit // 4) * 2 + (y + unit // 2) % 2
        return slot, unit % 2, flags

    def send(kind, slot, half, dest):
        return pltpu.make_async_remote_copy(
            src_ref=x.at[slot, half],
            dst_ref=x.at[slot, half],
            send_sem=send_sem.at[kind, slot, half],
            recv_sem=recv_sem.at[slot, half],
            device_id={"tensor": dest},
            device_id_type=pl.DeviceIdType.MESH,
        )

    def passed_on(slot, half, flags):
        near = (z // 2) * 2 + (1 - z % 2)
        return (
            (flags % 2 == 1, send(0, slot, half, me + 2)),
            (flags // 2 % 2 == 1, send(1, slot, half, me - 2)),
            (flags // 4 % 2 == 1, send(2, slot, half, z * 2 + 1 - y)),
            (flags // 8 % 2 == 1, send(3, z * 2 + 1 - y, 0, near * 2 + y)),
        )

    def forward(i):
        slot, half, flags = decode(i)
        for wanted, copy in passed_on(slot, half, flags):
            pl.when(wanted)(copy.start)

    forward(jnp.int32(0))
    forward(jnp.int32(1))

    loads[0].wait()
    eye = (
        lax.broadcasted_iota(jnp.int32, (128, 128), 0)
        == lax.broadcasted_iota(jnp.int32, (128, 128), 1)
    ).astype(jnp.bfloat16)

    def turn(j, carry):
        block = ad[core, pl.ds(pl.multiple_of(j * width, width), width), :]
        up_send[j] = dot_t(eye, block)[ADAPTER_RANK:, :].astype(jnp.bfloat16)
        return carry

    lax.fori_loop(0, 8, turn, 0)

    def up_copy(k):
        return pltpu.make_async_remote_copy(
            src_ref=up_send.at[(me + k) % 8],
            dst_ref=up_all.at[core, me],
            send_sem=up_ssem.at[k],
            recv_sem=up_rsem.at[k],
            device_id={"tensor": (me + k) % 8},
            device_id_type=pl.DeviceIdType.MESH,
        )

    for k in range(1, 8):
        up_copy(k).start()
    up_own = pltpu.make_async_copy(up_send.at[me], up_all.at[core, me], local_sem.at[5])
    up_own.start()

    q_out[...] = jnp.zeros_like(q_out)
    kv_out[...] = jnp.zeros_like(kv_out)
    low_out[...] = jnp.zeros_like(low_out)
    loads[1].wait()
    loads[2].wait()

    def work(i, carry):
        slot, half, flags = decode(i)

        @pl.when(i >= 2)
        def _():
            send(0, slot, half, me).wait_recv()
            for wanted, copy in passed_on(slot, half, flags):
                pl.when(wanted)(copy.start)

        block = x[slot, half]
        depth = pl.ds(pl.multiple_of(slot * width, width), width)
        here = pl.ds(pl.multiple_of(half * rows, rows), rows)
        for c in range(0, q_out.shape[1], 256):
            q_out[here, c : c + 256] += jnp.dot(
                block, w[depth, c : c + 256], preferred_element_type=jnp.float32
            )
        kv_out[here, :] += jnp.dot(block, wk[depth, :], preferred_element_type=jnp.float32)

        @pl.when(half == 0)
        def _():
            for k in range(POOL_PER_INDEX):
                low_out[k] += jnp.dot(block, ad[k, depth, :], preferred_element_type=jnp.float32)

        return carry

    lax.fori_loop(0, 16, work, 0)

    up_own.wait()
    for k in range(1, 8):
        up_copy(k).wait()
    pair = pltpu.make_async_remote_copy(
        src_ref=up_all.at[core],
        dst_ref=up_all.at[core],
        send_sem=pair_sem.at[0],
        recv_sem=pair_sem.at[1],
        device_id={"section": 1 - core},
        device_id_type=pl.DeviceIdType.MESH,
    )
    pair.start()

    def drain(i, carry):
        slot, half, flags = decode(i)
        for wanted, copy in passed_on(slot, half, flags):
            pl.when(wanted)(copy.wait_send)
        return carry

    lax.fori_loop(0, 16, drain, 0)
    pair.wait()
    result = pltpu.make_async_copy(up_all, up_out, local_sem.at[6])
    result.start()
    result.wait()


def project(tokens, decode_hidden_rows, query_matrix, key_value_matrix, pool):
    rows, width = tokens.shape
    cols, kv_cols = query_matrix.shape[1], key_value_matrix.shape[1]
    depth = query_matrix.shape[0]
    bf16, f32 = jnp.bfloat16, jnp.float32
    whole = pl.BlockSpec(memory_space=pltpu.VMEM)
    return pl.pallas_call(
        project_kernel,
        in_specs=[pl.BlockSpec(memory_space=pl.ANY)] * 5,
        out_specs=[whole, whole, whole, pl.BlockSpec(memory_space=pl.ANY)],
        out_shape=[
            jax.ShapeDtypeStruct((2 * rows, cols), f32),
            jax.ShapeDtypeStruct((2 * rows, kv_cols), f32),
            jax.ShapeDtypeStruct((POOL_PER_INDEX, rows, 128), f32),
            jax.ShapeDtypeStruct((2, 8, ADAPTER_RANK, width), bf16),
        ],
        scratch_shapes=[
            pltpu.VMEM((8, 2, rows, width), bf16),
            pltpu.VMEM((depth, cols), bf16),
            pltpu.VMEM((depth, kv_cols), bf16),
            pltpu.VMEM(pool.shape, bf16),
            pltpu.VMEM((8, ADAPTER_RANK, width), bf16),
            pltpu.VMEM((2, 8, ADAPTER_RANK, width), bf16),
            pltpu.SemaphoreType.DMA((7,)),
            pltpu.SemaphoreType.DMA((4, 8, 2)),
            pltpu.SemaphoreType.DMA((8, 2)),
            pltpu.SemaphoreType.DMA((8,)),
            pltpu.SemaphoreType.DMA((8,)),
            pltpu.SemaphoreType.DMA((2,)),
        ],
        compiler_params=pltpu.CompilerParams(
            collective_id=0, has_side_effects=True, vmem_limit_bytes=60 * 1024 * 1024
        ),
        cost_estimate=pl.CostEstimate(
            flops=4 * rows * depth * (cols + kv_cols), bytes_accessed=30 << 20, transcendentals=0
        ),
    )(tokens, decode_hidden_rows, query_matrix, key_value_matrix, pool)


def live_bias(decode_page_table, lengths, page_count):
    match = decode_page_table[:, :, None] == jnp.arange(page_count, dtype=jnp.int32)[None, None, :]
    place = jnp.max(jnp.where(match, jnp.arange(PPR, dtype=jnp.int32)[None, :, None], -1), axis=1)
    left = jnp.where(place >= 0, lengths[:, None] - place * PAGE, 0)
    live = jnp.arange(PAGE, dtype=jnp.int32)[None, None, :] < left[:, :, None]
    bias = jnp.where(live, 0.0, -jnp.inf).astype(jnp.bfloat16)
    return bias.reshape(lengths.shape[0], page_count * PAGE)


def own_heads(keyval_mine, heads_here):
    index = lax.axis_index("tensor")
    if heads_here == GROUP and keyval_mine.shape[1] == 2 * HD:
        half = KVH // 2
        first, second = keyval_mine[:, :HD], keyval_mine[:, HD:]
        holds_keys = index < half
        one = lax.ppermute(
            jnp.where(holds_keys, first, second),
            "tensor",
            [(j, 2 * j) for j in range(half)] + [(half + j, 2 * j + 1) for j in range(half)],
        )
        two = lax.ppermute(
            jnp.where(holds_keys, second, first),
            "tensor",
            [(j, 2 * j + 1) for j in range(half)] + [(half + j, 2 * j) for j in range(half)],
        )
        even = index % 2 == 0
        return jnp.where(even, one, two), jnp.where(even, two, one)
    kv_here = max(1, heads_here // GROUP)
    whole = lax.all_gather(keyval_mine, "tensor", axis=1, tiled=True)
    first = index * heads_here // GROUP
    return (
        lax.dynamic_slice_in_dim(whole, first * HD, kv_here * HD, 1),
        lax.dynamic_slice_in_dim(whole, (KVH + first) * HD, kv_here * HD, 1),
    )


def on_device(
    tokens,
    decode_hidden_rows,
    query_matrix,
    key_value_matrix,
    adapter_slot_pool,
    adapter_slot_map,
    tenant_adapter_index,
    decode_page_table,
    lengths,
):
    token_rows = tokens.shape[0]
    heads_here = query_matrix.shape[1] // HD
    stretches = token_rows // CTOK
    index = lax.axis_index("tensor")
    slots = adapter_slot_map[tenant_adapter_index]

    linked = lax.axis_size("tensor") == 8 and lax.axis_size("section") == 2
    if linked and heads_here == GROUP:
        query_all, keyval_all, low_local, up_all = project(
            tokens, decode_hidden_rows, query_matrix, key_value_matrix, adapter_slot_pool
        )
        query_sum, query_dec = query_all[:token_rows], query_all[token_rows:]
        keyval_mine = keyval_all.astype(jnp.bfloat16)
        low_local = low_local[:, :, :ADAPTER_RANK]
        picked = up_all[slots % POOL_PER_INDEX, slots // POOL_PER_INDEX]
    else:
        up = jnp.swapaxes(adapter_slot_pool[:, :, ADAPTER_RANK:], 1, 2)
        up_all = lax.all_to_all(up, "tensor", split_axis=2, concat_axis=0, tiled=True)
        tokens_all = lax.all_gather(tokens, "tensor", axis=1, tiled=True)
        rows_all = lax.all_gather(decode_hidden_rows, "tensor", axis=1, tiled=True)

        low_local = jnp.einsum(
            "td,sdr->str",
            tokens_all,
            adapter_slot_pool[:, :, :ADAPTER_RANK],
            preferred_element_type=jnp.float32,
        )
        query_sum = jnp.dot(tokens_all, query_matrix, preferred_element_type=jnp.float32)
        keyval_tok = jnp.dot(tokens_all, key_value_matrix, preferred_element_type=jnp.float32)
        query_dec = jnp.dot(rows_all, query_matrix, preferred_element_type=jnp.float32)
        keyval_dec = jnp.dot(rows_all, key_value_matrix, preferred_element_type=jnp.float32)
        keyval_mine = jnp.concatenate((keyval_tok, keyval_dec), axis=0).astype(jnp.bfloat16)
        picked = up_all[slots]

    low_local = low_local.reshape(POOL_PER_INDEX, stretches, CTOK, ADAPTER_RANK)
    held = index * POOL_PER_INDEX + jnp.arange(POOL_PER_INDEX, dtype=jnp.int32)
    mine = held[:, None] == slots[None, :]
    low_mine = jnp.sum(jnp.where(mine[:, :, None, None], low_local, 0.0), axis=0)
    low = lax.psum(low_mine.astype(jnp.bfloat16), "tensor")
    update = jnp.einsum("ctr,crd->ctd", low, picked, preferred_element_type=jnp.float32)
    update = update.reshape(token_rows, query_matrix.shape[1])
    query_tok = (query_sum + ADAPTER_SCALE * update).astype(jnp.bfloat16)

    keys, vals = own_heads(keyval_mine, heads_here)
    keys_ctx = lax.all_gather(keys[:token_rows], "section", axis=0, tiled=True)
    vals_ctx = lax.all_gather(vals[:token_rows], "section", axis=0, tiled=True)
    bias = live_bias(decode_page_table, lengths, keys_ctx.shape[0] // PAGE)
    return tuple(
        attention(
            query_tok,
            query_dec.astype(jnp.bfloat16),
            keys[:token_rows],
            vals[:token_rows],
            keys_ctx,
            vals_ctx,
            keys[token_rows:],
            vals[token_rows:],
            bias,
        )
    )


def solution(mesh):
    placed = (
        P(("parts", "section"), "tensor"),
        P(("parts", "section"), "tensor"),
        P(None, "tensor"),
        P(None, "tensor"),
        P("tensor", None, None),
        P(),
        P(("parts", "section")),
        P(("parts", "section"), None),
        P(("parts", "section")),
    )
    return jax.shard_map(
        on_device,
        mesh=mesh,
        in_specs=placed,
        out_specs=(P(("parts", "section"), "tensor"), P(("parts", "section"), "tensor")),
        check_vma=False,
    )
```

```python
import functools
import math

import jax
import jax.numpy as jnp
from jax import lax
from jax.experimental import pallas as pl
from jax.experimental.pallas import tpu as pltpu
from jax.sharding import PartitionSpec as P

HQ = 64
KVH = 8
HD = 128
ADAPTER_RANK = 64
CTOK = 128
POOL_PER_INDEX = 2
PAGE = 16
PPR = 32
ADAPTER_SCALE = 2.0
SCALE = 1.0 / math.sqrt(HD)
GROUP = HQ // KVH


def dot_t(a, b):
    return lax.dot_general(a, b, (((1,), (1,)), ((), ())), preferred_element_type=jnp.float32)


def attention_kernel(qt, qd, kt, vt, kc, vc, ks, vs, bias, out_t, out_d):
    causal = lax.broadcasted_iota(jnp.int32, (CTOK, CTOK), 0) >= lax.broadcasted_iota(
        jnp.int32, (CTOK, CTOK), 1
    )
    for c in range(qt.shape[0] // CTOK):
        rows = pl.ds(c * CTOK, CTOK)
        scores = jnp.where(causal, dot_t(qt[rows, :], kt[rows, :]) * SCALE, -jnp.inf)
        expo = jnp.exp(scores - jnp.max(scores, axis=-1, keepdims=True))
        weights = (expo / jnp.sum(expo, axis=-1, keepdims=True)).astype(jnp.bfloat16)
        result = jnp.dot(weights, vt[rows, :], preferred_element_type=jnp.float32)
        out_t[rows, :] = result.astype(jnp.bfloat16)
    tile = min(128, qd.shape[0])
    for r in range(qd.shape[0] // tile):
        rows = pl.ds(r * tile, tile)
        query = qd[rows, :]
        scores = dot_t(query, kc[...]) * SCALE + bias[rows, :].astype(jnp.float32)
        own = (
            jnp.sum(
                query.astype(jnp.float32) * ks[rows, :].astype(jnp.float32), axis=-1, keepdims=True
            )
            * SCALE
        )
        top = jnp.maximum(jnp.max(scores, axis=-1, keepdims=True), own)
        expo = jnp.exp(scores - top)
        own_exp = jnp.exp(own - top)
        total = jnp.sum(expo, axis=-1, keepdims=True) + own_exp
        weights = (expo / total).astype(jnp.bfloat16)
        own_weight = (own_exp / total).astype(jnp.bfloat16).astype(jnp.float32)
        result = jnp.dot(weights, vc[...], preferred_element_type=jnp.float32)
        result = result + own_weight * vs[rows, :].astype(jnp.float32)
        out_d[rows, :] = result.astype(jnp.bfloat16)


def attention(query_tok, query_dec, keys_tok, vals_tok, keys_ctx, vals_ctx, self_k, self_v, bias):
    heads = query_tok.shape[1] // HD

    def per_head(rows):
        return pl.BlockSpec((rows, HD), lambda i: (0, i))

    def per_group(array):
        return pl.BlockSpec((array.shape[0], HD), lambda i: (0, i // GROUP))

    shared = (keys_tok, vals_tok, keys_ctx, vals_ctx, self_k, self_v)
    return pl.pallas_call(
        attention_kernel,
        grid=(heads,),
        in_specs=[
            per_head(query_tok.shape[0]),
            per_head(query_dec.shape[0]),
            *[per_group(a) for a in shared],
            pl.BlockSpec(bias.shape, lambda i: (0, 0)),
        ],
        out_specs=[per_head(query_tok.shape[0]), per_head(query_dec.shape[0])],
        out_shape=[
            jax.ShapeDtypeStruct(query_tok.shape, jnp.bfloat16),
            jax.ShapeDtypeStruct(query_dec.shape, jnp.bfloat16),
        ],
        compiler_params=pltpu.CompilerParams(vmem_limit_bytes=32 * 1024 * 1024),
    )(query_tok, query_dec, *shared, bias)


SHARED = (0, 2)
QUARTERS = 4


def link_orders():
    arrived = {z: {(z, 0, q): 0 for q in range(QUARTERS)} for z in range(4)}
    waiting = {(z, way): [] for z in range(4) for way in range(3)}
    sent = {z: [] for z in range(4)}

    def reach(z, unit, time):
        source, side, q = unit
        if side == 0:
            if source <= z < 3:
                waiting[z, 0].append((q, time, abs(source - z), unit))
            if source >= z > 0:
                waiting[z, 1].append((q, time, abs(source - z), unit))
            if not (source == (z ^ 1) and q in SHARED):
                waiting[z, 2].append((q, time, abs(source - z), unit))
        elif source == z and q in SHARED:
            waiting[z, 0 if (z ^ 1) > z else 1].append((q, time, 9, unit))

    for z in range(4):
        for q in range(QUARTERS):
            reach(z, (z, 0, q), 0)
    for time in range(64):
        landed = []
        for (z, way), queue in waiting.items():
            if queue:
                best = min(queue)
                queue.remove(best)
                unit = best[3]
                sent[z].append((time, way, unit))
                place = (z + 1, z - 1, z)[way]
                landed.append((place, (unit[0], 1, unit[2]) if way == 2 else unit))
        for place, unit in landed:
            arrived[place][unit] = time + 1
            reach(place, unit, time + 1)
    tables = []
    for z in range(4):
        order = sorted(arrived[z], key=lambda u: (arrived[z][u], u[2], u[1], abs(u[0] - z), u))
        times = [arrived[z][u] for u in order]
        issue = [[] for _ in order]
        for time, way, unit in sorted(sent[z]):
            early = max([0] + [i for i in range(len(order)) if times[i] <= time - 1])
            step = max(early, order.index(unit))
            issue[step].append(64 + way * 16 + unit[0] * 4 + unit[2] + 128 * unit[1])
        prefill_ready = max(order.index(u) for u in order if u[2] < 2)
        decode_ready = max(order.index(u) for u in order if u[2] == 2)
        jobs = []
        for j in range(JOBS):
            step = jobs[-1] + 1 if jobs else prefill_ready
            jobs.append(min(31, max(step, decode_ready) if j == 6 else step))
        units = [u[0] * 8 + u[1] * 4 + u[2] for u in order]
        done = [sum(at <= i for at in jobs) for i in range(32)]
        tables.append((units, issue, done))
    return tables


JOBS = 12


def serve_kernel(
    slot_core, slot_index, held, tok, dec, wq, wkv, pool, bias,
    out_t, out_d,
    x, w, wk, ad, acc, acc_kv, acc_low, up_send, up_all, query, kv_send, ctx, own_kv, low_send, low_all,
    local_sem, send_sem, recv_sem, up_ssem, up_rsem, pair_sem,
    kv_ssem, kv_rsem, kv_lsem, ctx_ssem, ctx_rsem, low_ssem, low_rsem,
):
    tables = link_orders()
    mesh_id = pl.DeviceIdType.MESH
    me = lax.axis_index("tensor")
    core = lax.axis_index("section")
    z, y = me // 2, me % 2
    rows, width = tok.shape
    part = x.shape[2]
    heads = wq.shape[1] // HD

    own = [
        pltpu.make_async_copy(
            (tok, dec)[q // 2].at[pl.ds(q % 2 * part, part), :], x.at[me, q], local_sem.at[q]
        )
        for q in range(QUARTERS)
    ]
    loads = [
        pltpu.make_async_copy(pool, ad, local_sem.at[4]),
        pltpu.make_async_copy(wkv, wk, local_sem.at[5]),
        pltpu.make_async_copy(wq, w, local_sem.at[6]),
    ]
    for copy in own + loads:
        copy.start()

    barrier = pltpu.get_barrier_semaphore()
    for k in range(1, 8):
        pl.semaphore_signal(
            barrier, inc=1, device_id={"tensor": (me + k) % 8}, device_id_type=mesh_id
        )
    pl.semaphore_signal(barrier, inc=1, device_id={"section": 1 - core}, device_id_type=mesh_id)
    pl.semaphore_wait(barrier, 8)
    for copy in own:
        copy.wait()

    def look(i, values):
        code = jnp.int32(0)
        flat = z * 32 + i
        for place in range(4):
            for step in range(32):
                if values[place][step]:
                    code = jnp.where(flat == place * 32 + step, values[place][step], code)
        return code

    most = max(len(issue) for _, issues, _ in tables for issue in issues)

    def send(way, slot, q, dest):
        return pltpu.make_async_remote_copy(
            src_ref=x.at[slot, q],
            dst_ref=x.at[slot, q],
            send_sem=send_sem.at[way, slot, q],
            recv_sem=recv_sem.at[slot, q],
            device_id={"tensor": dest},
            device_id_type=mesh_id,
        )

    def passed_on(i):
        out = []
        for group in range(0, most, 3):
            word = look(
                i,
                [
                    [sum(c << (8 * k) for k, c in enumerate(issue[group : group + 3])) for issue in issues]
                    for _, issues, _ in tables
                ],
            )
            for k in range(min(3, most - group)):
                code = word // (1 << (8 * k)) % 256
                way = code // 16 % 4
                side = code // 128
                slot = code // 4 % 4 * 2 + (y + side) % 2
                dest = jnp.where(way == 0, me + 2, jnp.where(way == 1, me - 2, z * 2 + 1 - y))
                out.append((code > 0, send(way, slot, code % 4, dest)))
        return out

    def forward(i):
        for wanted, copy in passed_on(i):
            pl.when(wanted)(copy.start)

    forward(jnp.int32(0))

    loads[0].wait()
    eye = (
        lax.broadcasted_iota(jnp.int32, (128, 128), 0)
        == lax.broadcasted_iota(jnp.int32, (128, 128), 1)
    ).astype(jnp.bfloat16)

    def turn(j, carry):
        block = ad[core, pl.ds(pl.multiple_of(j * width, width), width), :]
        up_send[j] = dot_t(eye, block)[ADAPTER_RANK:, :].astype(jnp.bfloat16)
        return carry

    lax.fori_loop(0, 8, turn, 0)

    def peer_copy(src, dst, ssem, rsem, k):
        return pltpu.make_async_remote_copy(
            src_ref=src,
            dst_ref=dst,
            send_sem=ssem.at[k],
            recv_sem=rsem.at[k],
            device_id={"tensor": (me + k) % 8},
            device_id_type=mesh_id,
        )

    def up_copy(k):
        return peer_copy(up_send.at[(me + k) % 8], up_all.at[core, me], up_ssem, up_rsem, k)

    def low_copy(k):
        return peer_copy(low_send, low_all.at[k], low_ssem, low_rsem, k)

    def to_core(ref, ssem, rsem):
        return pltpu.make_async_remote_copy(
            src_ref=ref,
            dst_ref=ref,
            send_sem=ssem,
            recv_sem=rsem,
            device_id={"section": 1 - core},
            device_id_type=mesh_id,
        )

    for k in range(1, 8):
        up_copy(k).start()
    up_own = pltpu.make_async_copy(up_send.at[me], up_all.at[core, me], local_sem.at[7])
    up_own.start()

    acc[...] = jnp.zeros_like(acc)
    acc_kv[...] = jnp.zeros_like(acc_kv)
    acc_low[...] = jnp.zeros_like(acc_low)
    loads[1].wait()
    loads[2].wait()

    kind = me // 4
    stages = ((0, rows), (rows, part), (rows + part, part))

    def kv_place(stage, which):
        first, count = stages[stage]
        if stage == 0:
            return ctx.at[core, which]
        return own_kv.at[which, pl.ds(first - rows, count), :]

    def kv_copies(stage):
        first, count = stages[stage]
        for h in range(2):
            dest = me % 4 * 2 + h
            src = kv_send.at[h, pl.ds(first, count), :]
            remote = pltpu.make_async_remote_copy(
                src_ref=src,
                dst_ref=kv_place(stage, kind),
                send_sem=kv_ssem.at[stage, h],
                recv_sem=kv_rsem.at[stage, kind],
                device_id={"tensor": dest},
                device_id_type=mesh_id,
            )
            local = pltpu.make_async_copy(src, kv_place(stage, kind), kv_lsem.at[stage])
            yield dest, remote, local

    def kv_start(stage):
        first, count = stages[stage]
        here = pl.ds(first, count)
        for h in range(2):
            kv_send[h, here, :] = acc_kv[here, h * HD : (h + 1) * HD].astype(jnp.bfloat16)
        for dest, remote, local in kv_copies(stage):
            pl.when(dest != me)(remote.start)

            @pl.when(dest == me)
            def _(local=local):
                local.start()
                local.wait()

    def kv_wait(stage):
        first, count = stages[stage]
        for which in range(2):
            arrival = pltpu.make_async_remote_copy(
                src_ref=kv_send.at[0, pl.ds(first, count), :],
                dst_ref=kv_place(stage, which),
                send_sem=kv_ssem.at[stage, 0],
                recv_sem=kv_rsem.at[stage, which],
                device_id={"tensor": me},
                device_id_type=mesh_id,
            )
            pl.when(which * 4 + me // 2 != me)(arrival.wait_recv)

    def tokens_send():
        kv_start(0)
        packed = []
        for c in range(rows // CTOK):
            here = pl.ds(c * CTOK, CTOK)
            low = jnp.zeros((CTOK, 128), jnp.float32)
            for k in range(POOL_PER_INDEX):
                r = k * (rows // CTOK) + c
                low = low + jnp.where(held[r : r + 1, :] > 0.0, acc_low[k, here, :], 0.0)
            packed.append(low)
        lane = lax.broadcasted_iota(jnp.int32, (CTOK, 128), 1)
        half = len(packed) // 2
        for c in range(half):
            other = pltpu.roll(packed[half + c], ADAPTER_RANK, 1)
            both = jnp.where(lane < ADAPTER_RANK, packed[c], other)
            low_send[pl.ds(c * CTOK, CTOK), :] = both.astype(jnp.bfloat16)
        for k in range(1, 8):
            low_copy(k).start()

    def tokens_receive():
        up_own.wait()
        for k in range(1, 8):
            up_copy(k).wait()
        pair = to_core(up_all.at[core], pair_sem.at[0], pair_sem.at[1])
        pair.start()
        kv_wait(0)
        to_core(ctx.at[core], ctx_ssem, ctx_rsem).start()
        low = low_send[...].astype(jnp.float32)
        for k in range(1, 8):
            low_copy(k).wait()
            low = low + low_all[k].astype(jnp.float32)
        low = low.astype(jnp.bfloat16)
        pair.wait()
        half = rows // CTOK // 2
        for c in range(rows // CTOK):
            piece = low[c % half * CTOK : (c % half + 1) * CTOK, :]
            piece = piece[:, c // half * ADAPTER_RANK : (c // half + 1) * ADAPTER_RANK]
            update = jnp.dot(
                piece, up_all[slot_core[c], slot_index[c]], preferred_element_type=jnp.float32
            )
            here = pl.ds(c * CTOK, CTOK)
            query[here, :] = (acc[here, :] + ADAPTER_SCALE * update).astype(jnp.bfloat16)

    causal = lax.broadcasted_iota(jnp.int32, (CTOK, CTOK), 0) >= lax.broadcasted_iota(
        jnp.int32, (CTOK, CTOK), 1
    )

    def prefill_head(head):
        cols = pl.ds(pl.multiple_of(head * HD, HD), HD)
        for c in range(rows // CTOK):
            here = pl.ds(c * CTOK, CTOK)
            scores = dot_t(query[here, cols], ctx[core, 0, here, :]) * SCALE
            scores = jnp.where(causal, scores, -jnp.inf)
            expo = jnp.exp(scores - jnp.max(scores, axis=-1, keepdims=True))
            weights = expo / jnp.sum(expo, axis=-1, keepdims=True)
            result = jnp.dot(
                weights.astype(jnp.bfloat16), ctx[core, 1, here, :], preferred_element_type=jnp.float32
            )
            out_t[here, cols] = result.astype(jnp.bfloat16)

    def decode_head(head, first):
        cols = pl.ds(pl.multiple_of(head * HD, HD), HD)
        tile = 128
        for r in range(first, first + part, tile):
            here = pl.ds(r, tile)
            q = acc[pl.ds(rows + r, tile), cols].astype(jnp.bfloat16)
            scores = []
            for s in range(2):
                mask = bias[here, s * rows : (s + 1) * rows].astype(jnp.float32)
                scores.append(dot_t(q, ctx[s, 0]) * SCALE + mask)
            self_k = own_kv[0, here, :].astype(jnp.float32)
            mine = jnp.sum(q.astype(jnp.float32) * self_k, axis=-1, keepdims=True) * SCALE
            top = jnp.max(jnp.maximum(scores[0], scores[1]), axis=-1, keepdims=True)
            top = jnp.maximum(top, mine)
            expo = [jnp.exp(score - top) for score in scores]
            mine = jnp.exp(mine - top)
            inverse = 1.0 / (jnp.sum(expo[0] + expo[1], axis=-1, keepdims=True) + mine)
            weight = (mine * inverse).astype(jnp.bfloat16).astype(jnp.float32)
            result = weight * own_kv[1, here, :].astype(jnp.float32)
            for s in range(2):
                result = result + jnp.dot(
                    (expo[s] * inverse).astype(jnp.bfloat16),
                    ctx[s, 1],
                    preferred_element_type=jnp.float32,
                )
            out_d[here, cols] = result.astype(jnp.bfloat16)

    def job(j, carry):
        pl.when(j == 0)(tokens_send)
        pl.when(j == 1)(tokens_receive)

        @pl.when(jnp.logical_and(j >= 2, j < 6))
        def _():
            prefill_head((j - 2) * 2)
            prefill_head((j - 2) * 2 + 1)

        pl.when(j == 6)(lambda: kv_start(1))

        @pl.when(j == 7)
        def _():
            kv_wait(1)
            to_core(ctx.at[core], ctx_ssem, ctx_rsem).wait()

        @pl.when(j >= 8)
        def _():
            decode_head((j - 8) * 2, 0)
            decode_head((j - 8) * 2 + 1, 0)

        return carry

    unit_table = [units for units, _, _ in tables]
    done_table = [done for _, _, done in tables]

    def work(i, done):
        unit = look(i, unit_table)
        slot, q = unit // 8 * 2 + (y + unit // 4) % 2, unit % 4

        pl.when(slot != me)(send(0, slot, q, me).wait_recv)
        pl.when(i > 0)(lambda: forward(i))

        block = x[slot, q]
        depth = pl.ds(pl.multiple_of(slot * width, width), width)
        here = pl.ds(pl.multiple_of(q * part, part), part)
        for c in range(0, acc.shape[1], 256):
            acc[here, c : c + 256] += jnp.dot(
                block, w[depth, c : c + 256], preferred_element_type=jnp.float32
            )
        acc_kv[here, :] += jnp.dot(block, wk[depth, :], preferred_element_type=jnp.float32)

        @pl.when(q < 2)
        def _():
            for k in range(POOL_PER_INDEX):
                acc_low[k, here, :] += jnp.dot(
                    block, ad[k, depth, :], preferred_element_type=jnp.float32
                )

        until = look(i, done_table)
        lax.fori_loop(done, until, job, 0)
        return until

    lax.fori_loop(0, 32, work, jnp.int32(0))

    kv_start(2)

    def drain(i, carry):
        for wanted, copy in passed_on(i):
            pl.when(wanted)(copy.wait_send)
        return carry

    lax.fori_loop(0, 32, drain, 0)
    kv_wait(2)

    def last(head, carry):
        decode_head(head, part)
        return carry

    lax.fori_loop(0, heads, last, 0)
    for stage in range(3):
        for dest, remote, local in kv_copies(stage):
            pl.when(dest != me)(remote.wait_send)


def serve(slots, held, tokens, decode_hidden_rows, query_matrix, key_value_matrix, pool, bias):
    rows, width = tokens.shape
    depth, cols = query_matrix.shape
    kv_cols = key_value_matrix.shape[1]
    bf16, f32 = jnp.bfloat16, jnp.float32
    vmem = pl.BlockSpec(memory_space=pltpu.VMEM)
    smem = pl.BlockSpec(memory_space=pltpu.SMEM)
    hbm = pl.BlockSpec(memory_space=pl.ANY)
    dma = pltpu.SemaphoreType.DMA
    return pl.pallas_call(
        serve_kernel,
        in_specs=[smem, smem, vmem] + [hbm] * 5 + [vmem],
        out_specs=[vmem, vmem],
        out_shape=[jax.ShapeDtypeStruct((rows, cols), bf16)] * 2,
        scratch_shapes=[
            pltpu.VMEM((8, QUARTERS, rows // 2, width), bf16),
            pltpu.VMEM((depth, cols), bf16),
            pltpu.VMEM((depth, kv_cols), bf16),
            pltpu.VMEM(pool.shape, bf16),
            pltpu.VMEM((2 * rows, cols), f32),
            pltpu.VMEM((2 * rows, kv_cols), f32),
            pltpu.VMEM((POOL_PER_INDEX, rows, 128), f32),
            pltpu.VMEM((8, ADAPTER_RANK, width), bf16),
            pltpu.VMEM((2, 8, ADAPTER_RANK, width), bf16),
            pltpu.VMEM((rows, cols), bf16),
            pltpu.VMEM((2, 2 * rows, HD), bf16),
            pltpu.VMEM((2, 2, rows, HD), bf16),
            pltpu.VMEM((2, rows, HD), bf16),
            pltpu.VMEM((rows // 2, 128), bf16),
            pltpu.VMEM((8, rows // 2, 128), bf16),
            dma((8,)),
            dma((3, 8, QUARTERS)),
            dma((8, QUARTERS)),
            dma((8,)),
            dma((8,)),
            dma((2,)),
            dma((3, 2)),
            dma((3, 2)),
            dma((3,)),
            dma,
            dma,
            dma((8,)),
            dma((8,)),
        ],
        compiler_params=pltpu.CompilerParams(
            collective_id=0, has_side_effects=True, vmem_limit_bytes=62 * 1024 * 1024
        ),
        cost_estimate=pl.CostEstimate(
            flops=4 * rows * depth * (cols + kv_cols), bytes_accessed=30 << 20, transcendentals=0
        ),
    )(
        slots % POOL_PER_INDEX, slots // POOL_PER_INDEX, held,
        tokens, decode_hidden_rows, query_matrix, key_value_matrix, pool, bias,
    )


def live_bias(decode_page_table, lengths, page_count):
    match = decode_page_table[:, :, None] == jnp.arange(page_count, dtype=jnp.int32)[None, None, :]
    place = jnp.max(jnp.where(match, jnp.arange(PPR, dtype=jnp.int32)[None, :, None], -1), axis=1)
    left = jnp.where(place >= 0, lengths[:, None] - place * PAGE, 0)
    live = jnp.arange(PAGE, dtype=jnp.int32)[None, None, :] < left[:, :, None]
    bias = jnp.where(live, 0.0, -jnp.inf).astype(jnp.bfloat16)
    return bias.reshape(lengths.shape[0], page_count * PAGE)


def own_heads(keyval_mine, heads_here):
    index = lax.axis_index("tensor")
    if heads_here == GROUP and keyval_mine.shape[1] == 2 * HD:
        half = KVH // 2
        first, second = keyval_mine[:, :HD], keyval_mine[:, HD:]
        holds_keys = index < half
        one = lax.ppermute(
            jnp.where(holds_keys, first, second),
            "tensor",
            [(j, 2 * j) for j in range(half)] + [(half + j, 2 * j + 1) for j in range(half)],
        )
        two = lax.ppermute(
            jnp.where(holds_keys, second, first),
            "tensor",
            [(j, 2 * j + 1) for j in range(half)] + [(half + j, 2 * j) for j in range(half)],
        )
        even = index % 2 == 0
        return jnp.where(even, one, two), jnp.where(even, two, one)
    kv_here = max(1, heads_here // GROUP)
    whole = lax.all_gather(keyval_mine, "tensor", axis=1, tiled=True)
    first = index * heads_here // GROUP
    return (
        lax.dynamic_slice_in_dim(whole, first * HD, kv_here * HD, 1),
        lax.dynamic_slice_in_dim(whole, (KVH + first) * HD, kv_here * HD, 1),
    )


def on_device(
    tokens,
    decode_hidden_rows,
    query_matrix,
    key_value_matrix,
    adapter_slot_pool,
    adapter_slot_map,
    tenant_adapter_index,
    decode_page_table,
    lengths,
):
    token_rows = tokens.shape[0]
    heads_here = query_matrix.shape[1] // HD
    stretches = token_rows // CTOK
    index = lax.axis_index("tensor")
    slots = adapter_slot_map[tenant_adapter_index]

    linked = lax.axis_size("tensor") == 8 and lax.axis_size("section") == 2
    if linked and heads_here == GROUP:
        bias = live_bias(decode_page_table, lengths, 2 * token_rows // PAGE)
        here = index * POOL_PER_INDEX + jnp.arange(POOL_PER_INDEX, dtype=jnp.int32)
        mine = (here[:, None] == slots[None, :]).astype(jnp.float32).reshape(-1, 1)
        mine = jnp.broadcast_to(mine, (mine.shape[0], 128))
        return tuple(
            serve(
                slots,
                mine,
                tokens,
                decode_hidden_rows,
                query_matrix,
                key_value_matrix,
                adapter_slot_pool,
                bias,
            )
        )

    up = jnp.swapaxes(adapter_slot_pool[:, :, ADAPTER_RANK:], 1, 2)
    up_all = lax.all_to_all(up, "tensor", split_axis=2, concat_axis=0, tiled=True)
    tokens_all = lax.all_gather(tokens, "tensor", axis=1, tiled=True)
    rows_all = lax.all_gather(decode_hidden_rows, "tensor", axis=1, tiled=True)

    low_local = jnp.einsum(
        "td,sdr->str",
        tokens_all,
        adapter_slot_pool[:, :, :ADAPTER_RANK],
        preferred_element_type=jnp.float32,
    )
    query_sum = jnp.dot(tokens_all, query_matrix, preferred_element_type=jnp.float32)
    keyval_tok = jnp.dot(tokens_all, key_value_matrix, preferred_element_type=jnp.float32)
    query_dec = jnp.dot(rows_all, query_matrix, preferred_element_type=jnp.float32)
    keyval_dec = jnp.dot(rows_all, key_value_matrix, preferred_element_type=jnp.float32)

    low_local = low_local.reshape(POOL_PER_INDEX, stretches, CTOK, ADAPTER_RANK)
    held = index * POOL_PER_INDEX + jnp.arange(POOL_PER_INDEX, dtype=jnp.int32)
    mine = held[:, None] == slots[None, :]
    low_mine = jnp.sum(jnp.where(mine[:, :, None, None], low_local, 0.0), axis=0)
    low = lax.psum(low_mine.astype(jnp.bfloat16), "tensor")
    update = jnp.einsum("ctr,crd->ctd", low, up_all[slots], preferred_element_type=jnp.float32)
    update = update.reshape(token_rows, query_matrix.shape[1])
    query_tok = (query_sum + ADAPTER_SCALE * update).astype(jnp.bfloat16)

    keyval_mine = jnp.concatenate((keyval_tok, keyval_dec), axis=0).astype(jnp.bfloat16)
    keys, vals = own_heads(keyval_mine, heads_here)
    keys_ctx = lax.all_gather(keys[:token_rows], "section", axis=0, tiled=True)
    vals_ctx = lax.all_gather(vals[:token_rows], "section", axis=0, tiled=True)
    bias = live_bias(decode_page_table, lengths, keys_ctx.shape[0] // PAGE)
    return tuple(
        attention(
            query_tok,
            query_dec.astype(jnp.bfloat16),
            keys[:token_rows],
            vals[:token_rows],
            keys_ctx,
            vals_ctx,
            keys[token_rows:],
            vals[token_rows:],
            bias,
        )
    )


def solution(mesh):
    placed = (
        P(("parts", "section"), "tensor"),
        P(("parts", "section"), "tensor"),
        P(None, "tensor"),
        P(None, "tensor"),
        P("tensor", None, None),
        P(),
        P(("parts", "section")),
        P(("parts", "section"), None),
        P(("parts", "section")),
    )
    return jax.shard_map(
        on_device,
        mesh=mesh,
        in_specs=placed,
        out_specs=(P(("parts", "section"), "tensor"), P(("parts", "section"), "tensor")),
        check_vma=False,
    )
```
